1024 devices in a mesh: group: 32 (over x, z_hi, core), tp: 32 (over z_lo, y).
Axes of the slice: x: 4, y: 4, z: 32 (z_hi: 4, z_lo: 8; z = z_hi * 8 + z_lo), core: 2. Of those that a mesh axis runs over, the one named last changes fastest.
Arguments:
- token_inputs: bfloat16 [2, 512, 16384], P(None, 'group', 'tp'), may hold values from -6 to 6
- frozen_weight: bfloat16 [16384, 53248], P('tp', 'group'), may hold values from -0.046875 to 0.046875
- adapter_down_weight: bfloat16 [16384, 64], P('tp', 'group'), may hold values from -0.046875 to 0.046875
- adapter_up_weight: bfloat16 [64, 53248], P('tp', 'group'), may hold values from -0.75 to 0.75
Outputs:
- hidden_up: float32 [2, 512, 53248], P(None, 'tp', 'group')
The draws below stay inside these ranges and needn't reach their ends.
All inputs are finite; a program needn't handle non-finite values.
Results may differ from the reference program's by a relative error of at most 0.0029.
Values may be sent and summed in bfloat16 or wider, within the bound.
No kernel may reach another device: no remote copies, remote signals or barrier semaphores. Data moves between devices by JAX's collectives and lax.ppermute only.
A program may use at most 32 MiB of HBM per device.

```python
import jax
import jax.numpy as jnp
from jax import lax

MODEL_WIDTH = 16384
HIDDEN_UNITS = 53248
UPDATE_RANK = 64
STEPS = 2
TOKENS = 512
N_GROUP = 32


def spiked(drawn, rng, source, target, shards_of, factor):
    owner, partner = [(jnp.arange(drawn.shape[position]) // (drawn.shape[position] // shards_of)).reshape([-1 if axis == position else 1 for axis in range(drawn.ndim)]) for position in (source, target)]
    chosen = jax.random.permutation(rng, shards_of)[partner]
    strong = (owner == chosen) | (owner == (partner + shards_of // 2) % shards_of)
    return jnp.where(strong, factor * drawn, drawn)


def level_of(own_key, shape, shards, smallest, largest):
    gain, own = 1.0, jax.random.fold_in(own_key, 6)
    for dim, parts in shards:
        draws = jnp.exp(jax.random.uniform(jax.random.fold_in(own, dim), (parts,), jnp.float32, smallest / len(shards), largest / len(shards)))
        gain = gain * jnp.repeat(draws, shape[dim] // parts).reshape([-1 if axis == dim else 1 for axis in range(len(shape))])
    return gain


def centred(stream_key, extent, deviation, reach, pieces=(), kind=jnp.bfloat16):
    entries = jax.random.normal(stream_key, extent, jnp.float32) * deviation
    if len(pieces) > 0:
        entries = level_of(stream_key, extent, pieces, -0.22, 0.18) * entries
    return jnp.clip(entries, min=-reach, max=reach).astype(kind)


def bell_draw_with(key, dims, scale, limit, cuts, heavy, held_as=jnp.bfloat16):
    array = scale * jax.random.normal(key, dims, jnp.float32)
    if cuts:
        array = array * level_of(key, dims, cuts, -0.22, 0.18)
    return jnp.clip(spiked(array, jax.random.fold_in(key, 3), *heavy), -limit, limit).astype(held_as)


def setup_inputs(seed: int = 0) -> dict:
    seeds = jax.random.split(jax.random.key(seed), 5)
    token_inputs = bell_draw_with(seeds[0], (STEPS, TOKENS, MODEL_WIDTH), 1.0, 6.0, ((1, 32), (2, 32)), (2, 1, 32, 2.75))
    frozen_weight = centred(seeds[1], (MODEL_WIDTH, HIDDEN_UNITS), MODEL_WIDTH ** -0.5, 0.046875, ((0, 32), (1, 32)))
    adapter_down_weight = centred(seeds[2], (MODEL_WIDTH, UPDATE_RANK), MODEL_WIDTH ** -0.5, 0.046875, ((0, 32), (1, 32)))
    adapter_up_weight = centred(seeds[3], (UPDATE_RANK, HIDDEN_UNITS), UPDATE_RANK ** -0.5, 0.75, ((0, 32), (1, 32)))
    return {"token_inputs": token_inputs, "frozen_weight": frozen_weight, "adapter_down_weight": adapter_down_weight, "adapter_up_weight": adapter_up_weight}


adapter_scale = 0.5


def reference(token_inputs, frozen_weight, adapter_down_weight, adapter_up_weight):
    column_tile = HIDDEN_UNITS // N_GROUP
    gathered_row_list = token_inputs.reshape(STEPS * TOKENS, MODEL_WIDTH)
    complete_down_factor = adapter_down_weight

    def one_block(index):
        initial_step = (index * column_tile).astype(jnp.int32)
        frozen_columns = lax.dynamic_slice_in_dim(frozen_weight, initial_step, column_tile, 1).astype(jnp.float32)
        adapter_up_columns = lax.dynamic_slice_in_dim(adapter_up_weight, initial_step, column_tile, 1)
        delta = jnp.dot(complete_down_factor, adapter_up_columns, preferred_element_type=jnp.float32)
        merged_weight = (frozen_columns + adapter_scale * delta).astype(jnp.bfloat16)
        return jnp.dot(gathered_row_list, merged_weight, preferred_element_type=jnp.float32)

    stacked = lax.map(one_block, jnp.arange(N_GROUP, dtype=jnp.int32))
    return jnp.transpose(stacked, (1, 0, 2)).reshape(STEPS, TOKENS, HIDDEN_UNITS)
```

```python
import functools

import jax
import jax.numpy as jnp
from jax import lax
from jax.experimental import pallas as pl
from jax.experimental.pallas import tpu as pltpu
from jax.sharding import Mesh, PartitionSpec as P

adapter_scale = 0.5
RANK = 64
AXES = ("x", "zh", "core", "zl", "y")
SIZES = (4, 4, 2, 8, 4)
VMEM = pl.BlockSpec(memory_space=pltpu.VMEM)
SMEM = pl.BlockSpec(memory_space=pltpu.SMEM)
NT = (((1,), (1,)), ((), ()))


def product_kernel(step, place, own_half, other_half, weight, kept, *sent):
    y, core = place[0], place[1]
    width = weight.shape[1]
    padded = jnp.concatenate(
        [half[:, :, :, 32:48, :].reshape(256, 512) for half in (own_half, other_half)]
    )
    wanted = lax.broadcasted_iota(jnp.int32, (RANK, 512), 0)
    held = lax.broadcasted_iota(jnp.int32, (RANK, 512), 1)
    pick = held == (wanted // 2) * 16 + wanted % 2
    down = jnp.dot(
        pick.astype(jnp.float32).astype(jnp.bfloat16), padded, preferred_element_type=jnp.float32
    ).astype(jnp.bfloat16)
    for distance in range(4):
        target = lax.rem(y + distance, 4)
        parity, source_core = target // 2, lax.rem(target, 2)
        rows = slice(16 * step, 16 * step + 16)
        mine = own_half[:, :, parity, rows, :].reshape(128, 512)
        theirs = other_half[:, :, parity, rows, :].reshape(128, 512)
        tokens = jnp.where(source_core == core, mine, theirs)
        wide = jnp.dot(tokens, weight[...], preferred_element_type=jnp.float32)
        low = lax.dot_general(tokens, down, NT, preferred_element_type=jnp.float32)
        place_out = kept if distance == 0 else sent[distance - 1]
        place_out[:, :width] = wide.astype(place_out.dtype)
        place_out[:, width:] = low.astype(place_out.dtype)


def products(step, place, own_half, other_half, weight):
    columns = weight.shape[1] + RANK
    return pl.pallas_call(
        functools.partial(product_kernel, step),
        out_shape=[jax.ShapeDtypeStruct((128, columns), jnp.float32)]
        + [jax.ShapeDtypeStruct((128, columns), jnp.bfloat16)] * 3,
        in_specs=[SMEM, VMEM, VMEM, VMEM],
        out_specs=[VMEM] * 4,
        compiler_params=pltpu.CompilerParams(vmem_limit_bytes=40 << 20),
        cost_estimate=pl.CostEstimate(
            flops=2 * 512 * 512 * columns, bytes_accessed=6 << 20, transcendentals=0
        ),
        name="products",
    )(place, own_half, other_half, weight)


def sum_y_kernel(place, kept, first, second, third, sent, own):
    sent[...] = (
        kept[...]
        + first[...].astype(jnp.float32)
        + second[...].astype(jnp.float32)
        + third[...].astype(jnp.float32)
    ).astype(sent.dtype)
    rows = pl.ds(pl.multiple_of(place[2] * 16, 16), 16)
    own[...] = (
        kept[rows, :]
        + first[rows, :].astype(jnp.float32)
        + second[rows, :].astype(jnp.float32)
        + third[rows, :].astype(jnp.float32)
    )


def sum_y(place, kept, received):
    rows, columns = kept.shape
    return pl.pallas_call(
        sum_y_kernel,
        out_shape=[
            jax.ShapeDtypeStruct((rows, columns), jnp.bfloat16),
            jax.ShapeDtypeStruct((16, columns), jnp.float32),
        ],
        in_specs=[SMEM] + [VMEM] * 4,
        out_specs=[VMEM] * 2,
        compiler_params=pltpu.CompilerParams(vmem_limit_bytes=40 << 20),
        cost_estimate=pl.CostEstimate(
            flops=4 * rows * columns, bytes_accessed=12 * rows * columns, transcendentals=0
        ),
        name="sum_y",
    )(place, kept, *received)


def finish_kernel(place, own0, got0, own1, got1, up, result):
    for step, (own, got) in enumerate(((own0, got0), (own1, got1))):
        total = own[...]
        for source in range(8):
            part = got[source].astype(jnp.float32)
            total = total + jnp.where(place[2] == source, jnp.zeros_like(part), part)
        width = up.shape[1]
        low = total[:, width : width + up.shape[0]]
        coarse = low.astype(jnp.bfloat16)
        fine = (low - coarse.astype(jnp.float32)).astype(jnp.bfloat16)
        update = jnp.dot(coarse, up[...], preferred_element_type=jnp.float32) + jnp.dot(
            fine, up[...], preferred_element_type=jnp.float32
        )
        result[step] = total[:, :width] + adapter_scale * update


def finish(place, own0, got0, own1, got1, up):
    return pl.pallas_call(
        finish_kernel,
        out_shape=jax.ShapeDtypeStruct((2, 16, up.shape[1]), jnp.float32),
        in_specs=[SMEM] + [VMEM] * 5,
        out_specs=VMEM,
        compiler_params=pltpu.CompilerParams(vmem_limit_bytes=40 << 20),
        name="finish",
    )(place, own0, got0, own1, got1, up)


def copies(block, count):
    return jnp.broadcast_to(block[None], (count,) + block.shape)


def ring(count, distance):
    return [(i, (i + distance) % count) for i in range(count)]


def local(token_inputs, frozen_weight, adapter_down_weight, adapter_up_weight):
    place = jnp.stack([lax.axis_index("y"), lax.axis_index("core"), lax.axis_index("zl")])
    place = place.astype(jnp.int32)

    rows = jnp.pad(adapter_down_weight.T, ((0, 14), (0, 0)))
    block = jnp.concatenate([token_inputs.reshape(32, 512), rows])
    block = lax.all_to_all(copies(block, 4), "zh", 0, 0, tiled=True)
    own_half = lax.all_to_all(copies(block, 4).reshape(16, 48, 512), "x", 0, 0, tiled=True)
    other_half = lax.ppermute(own_half, "core", [(0, 1), (1, 0)])
    own_half = own_half.reshape(4, 2, 2, 48, 512)
    other_half = other_half.reshape(4, 2, 2, 48, 512)

    kept, received = [], []
    for step in range(2):
        own, *sent = products(step, place, own_half, other_half, frozen_weight)
        kept.append(own)
        received.append(
            [lax.ppermute(sent[d - 1], "y", ring(4, d)) for d in (1, 2, 3)]
        )

    adapter_up_weight, kept[1] = lax.optimization_barrier((adapter_up_weight, kept[1]))
    up = lax.all_to_all(copies(adapter_up_weight, 32), ("zl", "y"), 0, 0, tiled=True)
    up = up.reshape(16, 2, 2, -1)
    first_core = place[1] == 0
    up = jnp.stack(
        [
            jnp.where(first_core, up[:, 0], up[:, 1]),
            jnp.where(first_core, up[:, 1], up[:, 0]),
        ]
    ).reshape(RANK, -1)

    summed = []
    for step in range(2):
        sent, own = sum_y(place, kept[step], received[step])
        got = lax.all_to_all(sent.reshape(8, 16, -1), "zl", 0, 0, tiled=True)
        summed += [own, got]
    return finish(place, *summed, up)


def solution(mesh):
    fine = Mesh(mesh.devices.reshape(SIZES), AXES)
    group, tp = ("x", "zh", "core"), ("zl", "y")
    placed = (P(None, group, tp), P(tp, group), P(tp, group), P(tp, group))
    return jax.shard_map(
        local, mesh=fine, in_specs=placed, out_specs=P(None, tp, group), check_vma=False
    )
```

```python
import jax
import jax.numpy as jnp
from jax import lax
from jax.experimental import pallas as pl
from jax.experimental.pallas import tpu as pltpu
from jax.sharding import Mesh, PartitionSpec as P

adapter_scale = 0.5
RANK = 64
AXES = ("x", "zh", "core", "zp", "zb", "y")
SIZES = (4, 4, 2, 4, 2, 4)
VMEM = pl.BlockSpec(memory_space=pltpu.VMEM)
SMEM = pl.BlockSpec(memory_space=pltpu.SMEM)
NT = (((1,), (1,)), ((), ()))


def product_kernel(place, own_half, other_half, weight, sent, kept):
    me, core = place[0], place[1]
    width = weight.shape[1]
    padded = jnp.concatenate(
        [half[:, :, 32:48, :].reshape(256, 512) for half in (own_half, other_half)]
    )
    row = lax.broadcasted_iota(jnp.int32, (RANK, 512), 0)
    held = lax.broadcasted_iota(jnp.int32, (RANK, 512), 1)
    x = (row // 2 % 2) * 2 + row // 4 % 2
    zh = (row // 8 % 2) * 2 + row // 16 % 2
    pick = held == (row // 32) * 256 + (x * 4 + zh) * 16 + row % 2
    down = jnp.dot(
        pick.astype(jnp.float32).astype(jnp.bfloat16), padded, preferred_element_type=jnp.float32
    ).astype(jnp.bfloat16)
    for distance in range(8):
        target = lax.rem(me + distance, 8)
        zh, source_core = target // 2, lax.rem(target, 2)
        mine = own_half[:, zh, :32, :].reshape(128, 512)
        theirs = other_half[:, zh, :32, :].reshape(128, 512)
        tokens = jnp.where(source_core == core, mine, theirs)
        wide = jnp.dot(tokens, weight[...], preferred_element_type=jnp.float32)
        low = lax.dot_general(tokens, down, NT, preferred_element_type=jnp.float32)
        sent[target, :, :width] = wide.astype(sent.dtype)
        low = jnp.concatenate([low, jnp.zeros_like(low)], axis=1)
        sent[target, :, width:] = low.astype(sent.dtype)
        if distance == 0:
            kept[:, :width] = wide
            kept[:, width:] = low


def products(place, own_half, other_half, weight):
    columns = weight.shape[1] + 2 * RANK
    return pl.pallas_call(
        product_kernel,
        out_shape=[
            jax.ShapeDtypeStruct((8, 128, columns), jnp.bfloat16),
            jax.ShapeDtypeStruct((128, columns), jnp.float32),
        ],
        in_specs=[SMEM, VMEM, VMEM, VMEM],
        out_specs=[VMEM] * 2,
        compiler_params=pltpu.CompilerParams(vmem_limit_bytes=40 << 20),
        cost_estimate=pl.CostEstimate(
            flops=2 * 1024 * 512 * columns, bytes_accessed=8 << 20, transcendentals=0
        ),
        name="products",
    )(place, own_half, other_half, weight)


def total_of(own, got, me):
    total = own
    for source in range(got.shape[0]):
        part = got[source].astype(jnp.float32)
        total = total + jnp.where(me == source, jnp.zeros_like(part), part)
    return total


def first_sum_kernel(place, kept, got, sent, own):
    for pair in range(4):
        rows = slice(32 * pair, 32 * pair + 32)
        total = total_of(kept[rows, :], got.at[:, rows, :], place[0])
        sent[pair] = total.astype(sent.dtype)

        @pl.when(place[2] == pair)
        def _():
            own[...] = total


def first_sum(place, kept, got):
    columns = kept.shape[1]
    return pl.pallas_call(
        first_sum_kernel,
        out_shape=[
            jax.ShapeDtypeStruct((4, 32, columns), jnp.bfloat16),
            jax.ShapeDtypeStruct((32, columns), jnp.float32),
        ],
        in_specs=[SMEM] + [VMEM] * 2,
        out_specs=[VMEM] * 2,
        compiler_params=pltpu.CompilerParams(vmem_limit_bytes=40 << 20),
        name="first_sum",
    )(place, kept, got)


def finish_kernel(place, own, got, up, result):
    width = up.shape[1]
    total = total_of(own[...], got, place[2])
    low = total[:, width : width + RANK]
    coarse = low.astype(jnp.bfloat16)
    fine = (low - coarse.astype(jnp.float32)).astype(jnp.bfloat16)
    update = jnp.dot(coarse, up[...], preferred_element_type=jnp.float32) + jnp.dot(
        fine, up[...], preferred_element_type=jnp.float32
    )
    result[...] = (total[:, :width] + adapter_scale * update).reshape(result.shape)


def finish(place, own, got, up):
    return pl.pallas_call(
        finish_kernel,
        out_shape=jax.ShapeDtypeStruct((2, 16, up.shape[1]), jnp.float32),
        in_specs=[SMEM] + [VMEM] * 3,
        out_specs=VMEM,
        compiler_params=pltpu.CompilerParams(vmem_limit_bytes=40 << 20),
        name="finish",
    )(place, own, got, up)


def copies(block, count):
    return jnp.broadcast_to(block[None], (count,) + block.shape)


def doubled(block, axis, bit, first):
    other = lax.ppermute(block, axis, [(i, i ^ bit) for i in range(lax.axis_size(axis))])
    in_front = (lax.axis_index(axis) & bit) == first * bit
    return jnp.concatenate([jnp.where(in_front, block, other), jnp.where(in_front, other, block)])


def local(token_inputs, frozen_weight, adapter_down_weight, adapter_up_weight):
    core = lax.axis_index("core")
    place = jnp.stack([lax.axis_index(("zb", "y")), core, lax.axis_index("zp")])
    place = place.astype(jnp.int32)

    rows = jnp.pad(adapter_down_weight.T, ((0, 14), (0, 0)))
    block = jnp.concatenate([token_inputs.reshape(32, 512), rows])
    block = lax.all_to_all(copies(block, 4), "zh", 0, 0, tiled=True)
    own_half = lax.all_to_all(copies(block, 4).reshape(16, 48, 512), "x", 0, 0, tiled=True)
    other_half = lax.ppermute(own_half, "core", [(0, 1), (1, 0)])
    own_half = own_half.reshape(4, 4, 48, 512)
    other_half = other_half.reshape(4, 4, 48, 512)

    up = doubled(adapter_up_weight, "zp", 2, 0)
    up = doubled(up, "zp", 1, 0)
    up = doubled(up, "zb", 1, 0)

    sent, kept = products(place, own_half, other_half, frozen_weight)
    up, kept = lax.optimization_barrier((up, kept))
    got = lax.all_to_all(sent, ("zb", "y"), 0, 0, tiled=True)
    up = doubled(up, "y", 2, 0)
    up = doubled(up, "y", 1, core)
    up, got = lax.optimization_barrier((up, got))

    sent, own = first_sum(place, kept, got)
    got = lax.all_to_all(sent, "zp", 0, 0, tiled=True)
    return finish(place, own, got, up)


def solution(mesh):
    fine = Mesh(mesh.devices.reshape(SIZES), AXES)
    group, tp = ("x", "zh", "core"), ("zp", "zb", "y")
    placed = (P(None, group, tp), P(tp, group), P(tp, group), P(tp, group))
    return jax.shard_map(
        local, mesh=fine, in_specs=placed, out_specs=P(None, tp, group), check_vma=False
    )
```

```python
import jax
import jax.numpy as jnp
from jax import lax
from jax.experimental import pallas as pl
from jax.experimental.pallas import tpu as pltpu
from jax.sharding import Mesh, PartitionSpec as P

adapter_scale = 0.5
RANK = 64
AXES = ("x", "zh", "core", "zp", "zb", "y")
SIZES = (4, 4, 2, 4, 2, 4)
VMEM = pl.BlockSpec(memory_space=pltpu.VMEM)
ANY = pl.BlockSpec(memory_space=pl.ANY)
HBM = pl.BlockSpec(memory_space=pltpu.HBM)
SMEM = pl.BlockSpec(memory_space=pltpu.SMEM)
NT = (((1,), (1,)), ((), ()))


def product_kernel(
    place, own_half, other_half, up, weight_hbm, sent_hbm, kept, weight, sent, weight_sem, sent_sem
):
    me, core = place[0], place[1]
    width = weight.shape[1]
    loading = pltpu.make_async_copy(weight_hbm, weight, weight_sem)
    loading.start()
    gathered = jnp.concatenate(
        [half[:, :, 128:, :].reshape(128, 128) for half in (own_half, other_half)]
    )
    row = lax.broadcasted_iota(jnp.int32, (RANK, 256), 0)
    held = lax.broadcasted_iota(jnp.int32, (RANK, 256), 1)
    x = (row // 2 % 2) * 2 + row // 4 % 2
    zh = (row // 32) * 2 + row // 16 % 2
    other = jnp.where(row // 8 % 2 == core, 0, 1)
    first = other * 128 + (x * 4 + zh) * 8 + row % 2
    down = []
    for part in range(4):
        pick = (held == first + 2 * part).astype(jnp.float32).astype(jnp.bfloat16)
        down.append(jnp.dot(pick, gathered, preferred_element_type=jnp.float32))
    down = jnp.concatenate(down, axis=1).astype(jnp.bfloat16)
    for slot in range(2):
        sent[slot, 128:, :width] = up[...]
        sent[slot, 128:, width:] = jnp.zeros((8, sent.shape[2] - width), sent.dtype)
    loading.wait()

    leaving = [None, None]
    for distance in range(8):
        slot = distance % 2
        target = lax.rem(me + distance, 8)
        zh, source_core = target // 2, lax.rem(target, 2)
        mine = own_half[:, zh, :128, :]
        theirs = other_half[:, zh, :128, :]
        tokens = jnp.where(source_core == core, mine, theirs).reshape(4, 4, 32, 128)
        tokens = jnp.concatenate([tokens[:, part].reshape(128, 128) for part in range(4)], axis=1)
        if leaving[slot] is not None:
            leaving[slot].wait()
        wide = jnp.dot(tokens, weight[...], preferred_element_type=jnp.float32)
        low = lax.dot_general(tokens, down, NT, preferred_element_type=jnp.float32)
        low = jnp.concatenate([low, jnp.zeros_like(low)], axis=1)
        sent[slot, :128, :width] = wide.astype(sent.dtype)
        sent[slot, :128, width:] = low.astype(sent.dtype)
        leaving[slot] = pltpu.make_async_copy(sent.at[slot], sent_hbm.at[target], sent_sem.at[slot])
        leaving[slot].start()
        if distance == 0:
            kept[:, :width] = wide
            kept[:, width:] = low
    leaving[0].wait()
    leaving[1].wait()


def products(place, own_half, other_half, up, weight):
    columns = weight.shape[1] + 2 * RANK
    return pl.pallas_call(
        product_kernel,
        out_shape=[
            jax.ShapeDtypeStruct((8, 136, columns), jnp.bfloat16),
            jax.ShapeDtypeStruct((128, columns), jnp.float32),
        ],
        in_specs=[SMEM, VMEM, VMEM, VMEM, HBM],
        out_specs=[ANY, VMEM],
        scratch_shapes=[
            pltpu.VMEM(weight.shape, weight.dtype),
            pltpu.VMEM((2, 136, columns), jnp.bfloat16),
            pltpu.SemaphoreType.DMA,
            pltpu.SemaphoreType.DMA((2,)),
        ],
        compiler_params=pltpu.CompilerParams(vmem_limit_bytes=40 << 20),
        cost_estimate=pl.CostEstimate(
            flops=2 * 1024 * 512 * columns, bytes_accessed=8 << 20, transcendentals=0
        ),
        name="products",
    )(place, own_half, other_half, up, weight)


def total_of(own, got, me):
    total = own
    for source in range(got.shape[0]):
        part = got[source].astype(jnp.float32)
        total = total + jnp.where(me == source, jnp.zeros_like(part), part)
    return total


def first_sum_kernel(place, kept, got, sent, own, up):
    for pair in range(4):
        rows = slice(32 * pair, 32 * pair + 32)
        total = total_of(kept[rows, :], got.at[:, rows, :], place[0])
        sent[pair] = total.astype(sent.dtype)

        @pl.when(place[2] == pair)
        def _():
            own[...] = total

    for source in range(0, 8, 2):
        both = [got[source + i, 128:, : up.shape[1]] for i in range(2)]
        up[8 * source : 8 * source + 16, :] = jnp.concatenate(both)


def first_sum(place, kept, got):
    columns = kept.shape[1]
    return pl.pallas_call(
        first_sum_kernel,
        out_shape=[
            jax.ShapeDtypeStruct((4, 32, columns), jnp.bfloat16),
            jax.ShapeDtypeStruct((32, columns), jnp.float32),
            jax.ShapeDtypeStruct((RANK, columns - 2 * RANK), jnp.bfloat16),
        ],
        in_specs=[SMEM] + [VMEM] * 2,
        out_specs=[VMEM] * 3,
        compiler_params=pltpu.CompilerParams(vmem_limit_bytes=40 << 20),
        name="first_sum",
    )(place, kept, got)


def finish_kernel(place, own, got, up, result):
    width = up.shape[1]
    total = total_of(own[...], got, place[2])
    low = total[:, width : width + RANK]
    coarse = low.astype(jnp.bfloat16)
    fine = (low - coarse.astype(jnp.float32)).astype(jnp.bfloat16)
    update = jnp.dot(coarse, up[...], preferred_element_type=jnp.float32) + jnp.dot(
        fine, up[...], preferred_element_type=jnp.float32
    )
    result[...] = (total[:, :width] + adapter_scale * update).reshape(result.shape)


def finish(place, own, got, up):
    return pl.pallas_call(
        finish_kernel,
        out_shape=jax.ShapeDtypeStruct((2, 16, up.shape[1]), jnp.float32),
        in_specs=[SMEM] + [VMEM] * 3,
        out_specs=VMEM,
        compiler_params=pltpu.CompilerParams(vmem_limit_bytes=40 << 20),
        name="finish",
    )(place, own, got, up)


def copies(block, count):
    return jnp.broadcast_to(block[None], (count,) + block.shape)


def doubled(block, axis, bit):
    other = lax.ppermute(block, axis, [(i, i ^ bit) for i in range(lax.axis_size(axis))])
    lower = (lax.axis_index(axis) & bit) == 0
    return jnp.concatenate([jnp.where(lower, block, other), jnp.where(lower, other, block)])


def lane_blocks(rows):
    return rows.reshape(-1, 4, 128).transpose(1, 0, 2).reshape(-1, 128)


def local(token_inputs, frozen_weight, adapter_down_weight, adapter_up_weight):
    core = lax.axis_index("core")
    place = jnp.stack([lax.axis_index(("zb", "y")), core, lax.axis_index("zp")])
    place = place.astype(jnp.int32)

    block = jnp.concatenate(
        [lane_blocks(token_inputs.reshape(32, 512)), lane_blocks(adapter_down_weight.T)]
    )
    block = lax.all_to_all(copies(block, 4), "zh", 0, 0, tiled=True)
    up = doubled(doubled(adapter_up_weight, "zp", 2), "zp", 1)
    block, up = lax.optimization_barrier((block, up))
    own_half = lax.all_to_all(copies(block, 4).reshape(16, 136, 128), "x", 0, 0, tiled=True)
    other_half = lax.ppermute(own_half, "core", [(0, 1), (1, 0)])
    own_half = own_half.reshape(4, 4, 136, 128)
    other_half = other_half.reshape(4, 4, 136, 128)

    sent, kept = products(place, own_half, other_half, up, frozen_weight)
    got = lax.all_to_all(sent, ("zb", "y"), 0, 0, tiled=True)
    sent, own, up = first_sum(place, kept, got)
    got = lax.all_to_all(sent, "zp", 0, 0, tiled=True)
    return finish(place, own, got, up)


def solution(mesh):
    fine = Mesh(mesh.devices.reshape(SIZES), AXES)
    group, tp = ("x", "zh", "core"), ("zp", "zb", "y")
    placed = (P(None, group, tp), P(tp, group), P(tp, group), P(tp, group))
    return jax.shard_map(
        local, mesh=fine, in_specs=placed, out_specs=P(None, tp, group), check_vma=False
    )
```

```python
import jax
import jax.numpy as jnp
from jax import lax
from jax.experimental import pallas as pl
from jax.experimental.pallas import tpu as pltpu
from jax.sharding import Mesh, PartitionSpec as P

adapter_scale = 0.5
RANK = 64
AXES = ("x", "zh", "core", "zp", "zb", "y")
SIZES = (4, 4, 2, 4, 2, 4)
VMEM = pl.BlockSpec(memory_space=pltpu.VMEM)
SMEM = pl.BlockSpec(memory_space=pltpu.SMEM)
TN = (((0,), (0,)), ((), ()))


def product_kernel(place, own_half, other_half, up, frozen, sent, kept, weight):
    me, core = place[0], place[1]
    gathered = jnp.concatenate(
        [half[:, :, 128:, :].reshape(128, 128) for half in (own_half, other_half)]
    )
    row = lax.broadcasted_iota(jnp.int32, (RANK, 256), 0)
    held = lax.broadcasted_iota(jnp.int32, (RANK, 256), 1)
    pair = row // 2
    source = (pair % 8) ^ me
    x = (place[2] - pair // 8) & 3
    other = (source % 2) ^ core
    first = other * 128 + (x * 4 + source // 2) * 8 + row % 2
    down = []
    for part in range(4):
        pick = (held == first + 2 * part).astype(jnp.float32).astype(jnp.bfloat16)
        down.append(jnp.dot(pick, gathered, preferred_element_type=jnp.float32))
    down = jnp.concatenate(down, axis=1).astype(jnp.bfloat16)
    for part in range(4):
        rows = slice(128 * part, 128 * part + 128)
        delta = lax.dot_general(down[:, rows], up[...], TN, preferred_element_type=jnp.float32)
        merged = frozen[rows, :].astype(jnp.float32) + adapter_scale * delta
        weight[rows, :] = merged.astype(weight.dtype)

    for distance in range(8):
        target = lax.rem(me + distance, 8)
        zh, source_core = target // 2, lax.rem(target, 2)
        mine = own_half[:, zh, :128, :]
        theirs = other_half[:, zh, :128, :]
        tokens = jnp.where(source_core == core, mine, theirs).reshape(4, 4, 32, 128)
        tokens = jnp.concatenate([tokens[:, part].reshape(128, 128) for part in range(4)], axis=1)
        wide = jnp.dot(tokens, weight[...], preferred_element_type=jnp.float32)
        sent[target] = wide.astype(sent.dtype)
        if distance == 0:
            kept[...] = wide


def products(place, own_half, other_half, up, weight):
    columns = weight.shape[1]
    return pl.pallas_call(
        product_kernel,
        out_shape=[
            jax.ShapeDtypeStruct((8, 128, columns), jnp.bfloat16),
            jax.ShapeDtypeStruct((128, columns), jnp.float32),
        ],
        in_specs=[SMEM] + [VMEM] * 4,
        out_specs=[VMEM] * 2,
        scratch_shapes=[pltpu.VMEM(weight.shape, weight.dtype)],
        compiler_params=pltpu.CompilerParams(vmem_limit_bytes=40 << 20),
        cost_estimate=pl.CostEstimate(
            flops=2 * 1024 * 512 * columns, bytes_accessed=8 << 20, transcendentals=0
        ),
        name="products",
    )(place, own_half, other_half, up, weight)


def total_of(own, got, me):
    total = own
    for source in range(got.shape[0]):
        part = got[source].astype(jnp.float32)
        total = total + jnp.where(me == source, jnp.zeros_like(part), part)
    return total


def first_sum_kernel(place, kept, got, sent, own):
    for pair in range(4):
        rows = slice(32 * pair, 32 * pair + 32)
        total = total_of(kept[rows, :], got.at[:, rows, :], place[0])
        sent[pair] = total.astype(sent.dtype)

        @pl.when(place[2] == pair)
        def _():
            own[...] = total


def first_sum(place, kept, got):
    columns = kept.shape[1]
    return pl.pallas_call(
        first_sum_kernel,
        out_shape=[
            jax.ShapeDtypeStruct((4, 32, columns), jnp.bfloat16),
            jax.ShapeDtypeStruct((32, columns), jnp.float32),
        ],
        in_specs=[SMEM] + [VMEM] * 2,
        out_specs=[VMEM] * 2,
        compiler_params=pltpu.CompilerParams(vmem_limit_bytes=40 << 20),
        name="first_sum",
    )(place, kept, got)


def finish_kernel(place, own, got, result):
    result[...] = total_of(own[...], got, place[2]).reshape(result.shape)


def finish(place, own, got):
    return pl.pallas_call(
        finish_kernel,
        out_shape=jax.ShapeDtypeStruct((2, 16, own.shape[1]), jnp.float32),
        in_specs=[SMEM] + [VMEM] * 2,
        out_specs=VMEM,
        compiler_params=pltpu.CompilerParams(vmem_limit_bytes=40 << 20),
        name="finish",
    )(place, own, got)


def copies(block, count):
    return jnp.broadcast_to(block[None], (count,) + block.shape)


def joined(block, axis, moves):
    return jnp.concatenate([block] + [lax.ppermute(block, axis, move) for move in moves])


def swap(count, bit):
    return [(i, i ^ bit) for i in range(count)]


def ring(count, distance):
    return [(i, (i + distance) % count) for i in range(count)]


def lane_blocks(rows):
    return rows.reshape(-1, 4, 128).transpose(1, 0, 2).reshape(-1, 128)


def local(token_inputs, frozen_weight, adapter_down_weight, adapter_up_weight):
    core = lax.axis_index("core")
    place = jnp.stack([lax.axis_index(("zb", "y")), core, lax.axis_index("zp")])
    place = place.astype(jnp.int32)

    block = jnp.concatenate(
        [lane_blocks(token_inputs.reshape(32, 512)), lane_blocks(adapter_down_weight.T)]
    )
    block = lax.all_to_all(copies(block, 4), "zh", 0, 0, tiled=True)
    up = joined(adapter_up_weight, "y", [swap(4, 1)])
    up = joined(up, "y", [swap(4, 2)])
    block, up = lax.optimization_barrier((block, up))
    up = joined(up, "zb", [swap(2, 1)])
    up = joined(up, "zp", [ring(4, distance) for distance in (1, 2, 3)])
    own_half = lax.all_to_all(copies(block, 4).reshape(16, 136, 128), "x", 0, 0, tiled=True)
    other_half = lax.ppermute(own_half, "core", [(0, 1), (1, 0)])
    own_half = own_half.reshape(4, 4, 136, 128)
    other_half = other_half.reshape(4, 4, 136, 128)

    sent, kept = products(place, own_half, other_half, up, frozen_weight)
    got = lax.all_to_all(sent, ("zb", "y"), 0, 0, tiled=True)
    sent, own = first_sum(place, kept, got)
    got = lax.all_to_all(sent, "zp", 0, 0, tiled=True)
    return finish(place, own, got)


def solution(mesh):
    fine = Mesh(mesh.devices.reshape(SIZES), AXES)
    group, tp = ("x", "zh", "core"), ("zp", "zb", "y")
    placed = (P(None, group, tp), P(tp, group), P(tp, group), P(tp, group))
    return jax.shard_map(
        local, mesh=fine, in_specs=placed, out_specs=P(None, tp, group), check_vma=False
    )
```

```python
import jax
import jax.numpy as jnp
from jax import lax
from jax.experimental import pallas as pl
from jax.experimental.pallas import tpu as pltpu
from jax.sharding import Mesh, PartitionSpec as P

adapter_scale = 0.5
RANK = 64
AXES = ("x", "zh", "core", "zp", "zb", "ya", "yb")
SIZES = (4, 4, 2, 4, 2, 2, 2)
HALF = 896
VMEM = pl.BlockSpec(memory_space=pltpu.VMEM)
SMEM = pl.BlockSpec(memory_space=pltpu.SMEM)
TN = (((0,), (0,)), ((), ()))


def product_kernel(place, own_half, other_half, up, frozen, partner, sent, kept, weight):
    me, core = place[0], place[1]
    odd = me % 2
    columns = pl.ds(pl.multiple_of(odd * (frozen.shape[1] - HALF), 128), HALF)
    row = lax.broadcasted_iota(jnp.int32, (RANK, 256), 0)
    held = lax.broadcasted_iota(jnp.int32, (RANK, 256), 1)
    pair = row // 2
    source = ((pair & 1) * 4 + (pair >> 3 & 1) * 2 + (pair >> 4)) ^ me
    x = (place[2] - (pair >> 1 & 3)) & 3
    other = (source % 2) ^ core
    first = other * 128 + (x * 4 + source // 2) * 8 + row % 2
    up_columns = up[:, columns]
    for features in range(2):
        gathered = jnp.concatenate(
            [half[:, features, :, 128:, :].reshape(128, 128) for half in (own_half, other_half)]
        )
        for part in range(4):
            pick = (held == first + 2 * part).astype(jnp.float32).astype(jnp.bfloat16)
            down = jnp.dot(pick, gathered, preferred_element_type=jnp.float32).astype(jnp.bfloat16)
            delta = lax.dot_general(down, up_columns, TN, preferred_element_type=jnp.float32)
            rows = slice(128 * part, 128 * part + 128)
            held_rows = jnp.where(odd == features, frozen[rows, columns], partner[rows, :])
            merged = held_rows.astype(jnp.float32) + adapter_scale * delta
            start = 512 * features + 128 * part
            weight[start : start + 128, :] = merged.astype(weight.dtype)

    for distance in range(8):
        target = lax.rem(me + distance, 8)
        zh, source_core = target // 2, lax.rem(target, 2)
        tokens = []
        for features in range(2):
            mine = own_half[:, features, zh, :128, :]
            theirs = other_half[:, features, zh, :128, :]
            chosen = jnp.where(source_core == core, mine, theirs).reshape(4, 4, 32, 128)
            tokens += [chosen[:, part].reshape(128, 128) for part in range(4)]
        tokens = jnp.concatenate(tokens, axis=1)
        wide = jnp.dot(tokens, weight[...], preferred_element_type=jnp.float32)
        sent[target] = wide.astype(sent.dtype)
        if distance == 0:
            kept[...] = wide


def products(place, own_half, other_half, up, frozen, partner):
    return pl.pallas_call(
        product_kernel,
        out_shape=[
            jax.ShapeDtypeStruct((8, 128, HALF), jnp.bfloat16),
            jax.ShapeDtypeStruct((128, HALF), jnp.float32),
        ],
        in_specs=[SMEM] + [VMEM] * 5,
        out_specs=[VMEM] * 2,
        scratch_shapes=[pltpu.VMEM((1024, HALF), frozen.dtype)],
        compiler_params=pltpu.CompilerParams(vmem_limit_bytes=40 << 20),
        cost_estimate=pl.CostEstimate(
            flops=2 * 1024 * 1024 * HALF, bytes_accessed=8 << 20, transcendentals=0
        ),
        name="products",
    )(place, own_half, other_half, up, frozen, partner)


def total_of(own, got, me):
    total = own
    for source in range(got.shape[0]):
        part = got[source].astype(jnp.float32)
        total = total + jnp.where(me == source, jnp.zeros_like(part), part)
    return total


def first_sum_kernel(place, kept, got, sent, own):
    me = place[0]
    width = sent.shape[2]
    for pair in range(4):
        rows = slice(32 * pair, 32 * pair + 32)
        for odd in range(2):
            lanes = slice(2 * HALF - width, HALF) if odd else slice(0, HALF)
            total = jnp.where(me % 2 == odd, kept[rows, lanes], 0.0)
            for source in range(odd, 8, 2):
                part = got[source, rows, lanes].astype(jnp.float32)
                total = total + jnp.where(me == source, jnp.zeros_like(part), part)
            columns = slice(HALF, width) if odd else slice(0, HALF)
            sent[pair, :, columns] = total.astype(sent.dtype)

            @pl.when(place[2] == pair)
            def _():
                own[:, columns] = total


def first_sum(place, kept, got, columns):
    return pl.pallas_call(
        first_sum_kernel,
        out_shape=[
            jax.ShapeDtypeStruct((4, 32, columns), jnp.bfloat16),
            jax.ShapeDtypeStruct((32, columns), jnp.float32),
        ],
        in_specs=[SMEM] + [VMEM] * 2,
        out_specs=[VMEM] * 2,
        compiler_params=pltpu.CompilerParams(vmem_limit_bytes=40 << 20),
        name="first_sum",
    )(place, kept, got)


def finish_kernel(place, own, got, result):
    result[...] = total_of(own[...], got, place[2]).reshape(result.shape)


def finish(place, own, got):
    return pl.pallas_call(
        finish_kernel,
        out_shape=jax.ShapeDtypeStruct((2, 16, own.shape[1]), jnp.float32),
        in_specs=[SMEM] + [VMEM] * 2,
        out_specs=VMEM,
        compiler_params=pltpu.CompilerParams(vmem_limit_bytes=40 << 20),
        name="finish",
    )(place, own, got)


def copies(block, count):
    return jnp.broadcast_to(block[None], (count,) + block.shape)


def joined(block, axis, moves):
    return jnp.concatenate([block] + [lax.ppermute(block, axis, move) for move in moves])


def swap(count, bit):
    return [(i, i ^ bit) for i in range(count)]


def ring(count, distance):
    return [(i, (i + distance) % count) for i in range(count)]


def lane_blocks(rows):
    return rows.reshape(-1, 4, 128).transpose(1, 0, 2).reshape(-1, 128)


def local(token_inputs, frozen_weight, adapter_down_weight, adapter_up_weight):
    core, odd = lax.axis_index("core"), lax.axis_index("yb")
    place = jnp.stack([lax.axis_index(("zb", "ya", "yb")), core, lax.axis_index("zp")])
    place = place.astype(jnp.int32)
    width = frozen_weight.shape[1]

    block = jnp.concatenate(
        [lane_blocks(token_inputs.reshape(32, 512)), lane_blocks(adapter_down_weight.T)]
    )
    block = copies(block, 4)
    block, up = lax.optimization_barrier((block, adapter_up_weight))
    block = lax.all_to_all(block, "zh", 0, 0, tiled=True)
    away = lax.dynamic_slice_in_dim(frozen_weight, (1 - odd) * (width - HALF), HALF, 1)
    partner = lax.ppermute(away, "yb", swap(2, 1))
    up = joined(up, "zb", [swap(2, 1)])
    up = joined(up, "zp", [ring(4, distance) for distance in (1, 2, 3)])
    up = joined(up, "ya", [swap(2, 1)])
    up = joined(up, "yb", [swap(2, 1)])
    block, up, partner = lax.optimization_barrier((block, up, partner))
    own_half = lax.all_to_all(copies(block, 8).reshape(32, 136, 128), ("x", "yb"), 0, 0, tiled=True)
    other_half = lax.ppermute(own_half, "core", swap(2, 1))
    own_half = own_half.reshape(4, 2, 4, 136, 128)
    other_half = other_half.reshape(4, 2, 4, 136, 128)

    sent, kept = products(place, own_half, other_half, up, frozen_weight, partner)
    got = lax.all_to_all(sent, ("zb", "ya", "yb"), 0, 0, tiled=True)
    sent, own = first_sum(place, kept, got, width)
    got = lax.all_to_all(sent, "zp", 0, 0, tiled=True)
    return finish(place, own, got)


def solution(mesh):
    fine = Mesh(mesh.devices.reshape(SIZES), AXES)
    group, tp = ("x", "zh", "core"), ("zp", "zb", "ya", "yb")
    placed = (P(None, group, tp), P(tp, group), P(tp, group), P(tp, group))
    return jax.shard_map(
        local, mesh=fine, in_specs=placed, out_specs=P(None, tp, group), check_vma=False
    )
```

```python
import jax
import jax.numpy as jnp
from jax import lax
from jax.experimental import pallas as pl
from jax.experimental.pallas import tpu as pltpu
from jax.sharding import Mesh, PartitionSpec as P

adapter_scale = 0.5
RANK = 64
AXES = ("x", "zh", "core", "zp", "zb", "ya", "yb")
SIZES = (4, 4, 2, 4, 2, 2, 2)
HALF = 896
VMEM = pl.BlockSpec(memory_space=pltpu.VMEM)
SMEM = pl.BlockSpec(memory_space=pltpu.SMEM)
TN = (((0,), (0,)), ((), ()))


def product_kernel(place, own_half, other_half, up, frozen, partner, sent, kept, weight):
    me, core = place[0], place[1]
    odd = me % 2
    columns = pl.ds(pl.multiple_of(odd * (frozen.shape[1] - HALF), 128), HALF)
    row = lax.broadcasted_iota(jnp.int32, (RANK, 256), 0)
    held = lax.broadcasted_iota(jnp.int32, (RANK, 256), 1)
    pair = row >> 1
    source = (pair & 7) ^ me
    x = (place[2] - (pair >> 3)) & 3
    other = (source & 1) ^ core
    first = other * 128 + (x * 4 + (source >> 1)) * 8 + (row & 1)
    picks = [(held == first + 2 * part).astype(jnp.float32).astype(jnp.bfloat16) for part in range(4)]
    up_columns = up[:, columns]
    for whose in range(2):
        features = odd if whose == 0 else 1 - odd
        gathered = jnp.concatenate(
            [half[:, features, :, 128:, :].reshape(128, 128) for half in (own_half, other_half)]
        )
        for part in range(4):
            down = jnp.dot(picks[part], gathered, preferred_element_type=jnp.float32)
            down = down.astype(jnp.bfloat16)
            delta = lax.dot_general(down, up_columns, TN, preferred_element_type=jnp.float32)
            rows = slice(128 * part, 128 * part + 128)
            before = frozen[rows, columns] if whose == 0 else partner[rows, :]
            merged = before.astype(jnp.float32) + adapter_scale * delta
            start = pl.multiple_of(512 * features + 128 * part, 128)
            weight[pl.ds(start, 128), :] = merged.astype(weight.dtype)

    for zh in range(4):
        for other, half in enumerate((own_half, other_half)):
            target = zh * 2 + (core ^ other)
            tokens = []
            for features in range(2):
                block = half[:, features, zh, :128, :].reshape(4, 4, 32, 128)
                tokens += [block[:, part].reshape(128, 128) for part in range(4)]
            tokens = jnp.concatenate(tokens, axis=1)
            wide = jnp.dot(tokens, weight[...], preferred_element_type=jnp.float32)
            sent[target] = wide.astype(sent.dtype)

            @pl.when(target == me)
            def _():
                kept[...] = wide


def products(place, own_half, other_half, up, frozen, partner):
    return pl.pallas_call(
        product_kernel,
        out_shape=[
            jax.ShapeDtypeStruct((8, 128, HALF), jnp.bfloat16),
            jax.ShapeDtypeStruct((128, HALF), jnp.float32),
        ],
        in_specs=[SMEM] + [VMEM] * 5,
        out_specs=[VMEM] * 2,
        scratch_shapes=[pltpu.VMEM((1024, HALF), frozen.dtype)],
        compiler_params=pltpu.CompilerParams(vmem_limit_bytes=20 << 20),
        cost_estimate=pl.CostEstimate(
            flops=2 * 1024 * 1024 * HALF, bytes_accessed=8 << 20, transcendentals=0
        ),
        name="products",
    )(place, own_half, other_half, up, frozen, partner)


def total_of(own, got, me):
    total = own
    for source in range(got.shape[0]):
        part = got[source].astype(jnp.float32)
        total = total + jnp.where(me == source, jnp.zeros_like(part), part)
    return total


def first_sum_kernel(place, kept, got, sent, own):
    me = place[0]
    width = sent.shape[2]
    for pair in range(4):
        rows = slice(32 * pair, 32 * pair + 32)
        for odd in range(2):
            lanes = slice(2 * HALF - width, HALF) if odd else slice(0, HALF)
            total = jnp.where(me % 2 == odd, kept[rows, lanes], 0.0)
            for source in range(odd, 8, 2):
                part = got[source, rows, lanes].astype(jnp.float32)
                total = total + jnp.where(me == source, jnp.zeros_like(part), part)
            columns = slice(HALF, width) if odd else slice(0, HALF)
            sent[pair, :, columns] = total.astype(sent.dtype)

            @pl.when(place[2] == pair)
            def _():
                own[:, columns] = total


def first_sum(place, kept, got, columns):
    return pl.pallas_call(
        first_sum_kernel,
        out_shape=[
            jax.ShapeDtypeStruct((4, 32, columns), jnp.bfloat16),
            jax.ShapeDtypeStruct((32, columns), jnp.float32),
        ],
        in_specs=[SMEM] + [VMEM] * 2,
        out_specs=[VMEM] * 2,
        compiler_params=pltpu.CompilerParams(vmem_limit_bytes=20 << 20),
        name="first_sum",
    )(place, kept, got)


def finish_kernel(place, own, got, result):
    result[...] = total_of(own[...], got, place[2]).reshape(result.shape)


def finish(place, own, got):
    return pl.pallas_call(
        finish_kernel,
        out_shape=jax.ShapeDtypeStruct((2, 16, own.shape[1]), jnp.float32),
        in_specs=[SMEM] + [VMEM] * 2,
        out_specs=VMEM,
        compiler_params=pltpu.CompilerParams(vmem_limit_bytes=20 << 20),
        name="finish",
    )(place, own, got)


def copies(block, count):
    return jnp.broadcast_to(block[None], (count,) + block.shape)


def joined(block, axis, moves):
    return jnp.concatenate([block] + [lax.ppermute(block, axis, move) for move in moves])


def swap(count, bit):
    return [(i, i ^ bit) for i in range(count)]


def ring(count, distance):
    return [(i, (i + distance) % count) for i in range(count)]


def lane_blocks(rows):
    return rows.reshape(-1, 4, 128).transpose(1, 0, 2).reshape(-1, 128)


def local(token_inputs, frozen_weight, adapter_down_weight, adapter_up_weight):
    core, odd = lax.axis_index("core"), lax.axis_index("yb")
    place = jnp.stack([lax.axis_index(("zb", "ya", "yb")), core, lax.axis_index("zp")])
    place = place.astype(jnp.int32)
    width = frozen_weight.shape[1]

    block = jnp.concatenate(
        [lane_blocks(token_inputs.reshape(32, 512)), lane_blocks(adapter_down_weight.T)]
    )
    block = copies(block, 4)
    block, up = lax.optimization_barrier((block, adapter_up_weight))
    block = lax.all_to_all(block, "zh", 0, 0, tiled=True)
    away = lax.dynamic_slice_in_dim(frozen_weight, (1 - odd) * (width - HALF), HALF, 1)
    partner = lax.ppermute(away, "yb", swap(2, 1))
    up = joined(up, "yb", [swap(2, 1)])
    up = joined(up, "ya", [swap(2, 1)])
    up = joined(up, "zb", [swap(2, 1)])
    up = joined(up, "zp", [ring(4, distance) for distance in (1, 2, 3)])
    block, up, partner = lax.optimization_barrier((block, up, partner))
    own_half = lax.all_to_all(copies(block, 8).reshape(32, 136, 128), ("x", "yb"), 0, 0, tiled=True)
    other_half = lax.ppermute(own_half, "core", swap(2, 1))
    own_half = own_half.reshape(4, 2, 4, 136, 128)
    other_half = other_half.reshape(4, 2, 4, 136, 128)

    sent, kept = products(place, own_half, other_half, up, frozen_weight, partner)
    got = lax.all_to_all(sent, ("zb", "ya", "yb"), 0, 0, tiled=True)
    sent, own = first_sum(place, kept, got, width)
    got = lax.all_to_all(sent, "zp", 0, 0, tiled=True)
    return finish(place, own, got)


def solution(mesh):
    fine = Mesh(mesh.devices.reshape(SIZES), AXES)
    group, tp = ("x", "zh", "core"), ("zp", "zb", "ya", "yb")
    placed = (P(None, group, tp), P(tp, group), P(tp, group), P(tp, group))
    return jax.shard_map(
        local, mesh=fine, in_specs=placed, out_specs=P(None, tp, group), check_vma=False
    )
```

```python
import jax
import jax.numpy as jnp
from jax import lax
from jax.experimental import pallas as pl
from jax.experimental.pallas import tpu as pltpu
from jax.sharding import Mesh, PartitionSpec as P

adapter_scale = 0.5
RANK = 64
AXES = ("x", "zh", "core", "zp", "zb", "ya", "yb")
SIZES = (4, 4, 2, 4, 2, 2, 2)
HALF = 896
VMEM = pl.BlockSpec(memory_space=pltpu.VMEM)
SMEM = pl.BlockSpec(memory_space=pltpu.SMEM)
TN = (((0,), (0,)), ((), ()))


def product_kernel(place, own_half, other_half, up, frozen, partner, sent, weight):
    me, core = place[0], place[1]
    odd = me % 2
    columns = pl.ds(pl.multiple_of(odd * (frozen.shape[1] - HALF), 128), HALF)
    row = lax.broadcasted_iota(jnp.int32, (RANK, 256), 0)
    held = lax.broadcasted_iota(jnp.int32, (RANK, 256), 1)
    pair = row >> 1
    source = (pair & 7) ^ me
    x = (pair >> 3) ^ place[2]
    other = (source & 1) ^ core
    first = other * 128 + (x * 4 + (source >> 1)) * 8 + (row & 1)
    picks = [(held == first + 2 * part).astype(jnp.float32).astype(jnp.bfloat16) for part in range(4)]
    up_columns = up[:, columns]
    for whose in range(2):
        features = odd if whose == 0 else 1 - odd
        gathered = jnp.concatenate(
            [half[:, features, :, 128:, :].reshape(128, 128) for half in (own_half, other_half)]
        )
        for part in range(4):
            down = jnp.dot(picks[part], gathered, preferred_element_type=jnp.float32)
            down = down.astype(jnp.bfloat16)
            delta = lax.dot_general(down, up_columns, TN, preferred_element_type=jnp.float32)
            rows = slice(128 * part, 128 * part + 128)
            before = frozen[rows, columns] if whose == 0 else partner[rows, :]
            merged = before.astype(jnp.float32) + adapter_scale * delta
            start = pl.multiple_of(512 * features + 128 * part, 128)
            weight[pl.ds(start, 128), :] = merged.astype(weight.dtype)

    for other, half in enumerate((own_half, other_half)):
        tokens = []
        for zh in range(4):
            lanes = []
            for features in range(2):
                block = half[:, features, zh, :128, :].reshape(4, 4, 32, 128)
                lanes += [block[:, part].reshape(128, 128) for part in range(4)]
            tokens.append(jnp.concatenate(lanes, axis=1))
        tokens = jnp.concatenate(tokens)
        wide = jnp.dot(tokens, weight[...], preferred_element_type=jnp.float32)
        for zh in range(4):
            sent[zh * 2 + (core ^ other)] = wide[128 * zh : 128 * zh + 128, :].astype(sent.dtype)


def products(place, own_half, other_half, up, frozen, partner):
    return pl.pallas_call(
        product_kernel,
        out_shape=jax.ShapeDtypeStruct((8, 128, HALF), jnp.bfloat16),
        in_specs=[SMEM] + [VMEM] * 5,
        out_specs=VMEM,
        scratch_shapes=[pltpu.VMEM((1024, HALF), frozen.dtype)],
        compiler_params=pltpu.CompilerParams(vmem_limit_bytes=20 << 20),
        cost_estimate=pl.CostEstimate(
            flops=2 * 1024 * 1024 * HALF, bytes_accessed=8 << 20, transcendentals=0
        ),
        name="products",
    )(place, own_half, other_half, up, frozen, partner)


def first_sum_kernel(place, got, own, *sent):
    width = own.shape[1]
    for distance in range(4):
        rows = pl.ds(pl.multiple_of(((place[2] + distance) & 3) * 32, 32), 32)
        for odd in range(2):
            lanes = slice(2 * HALF - width, HALF) if odd else slice(0, HALF)
            total = got[odd, rows, lanes].astype(jnp.float32)
            for source in range(odd + 2, 8, 2):
                total = total + got[source, rows, lanes].astype(jnp.float32)
            columns = slice(HALF, width) if odd else slice(0, HALF)
            if distance == 0:
                own[:, columns] = total
            else:
                sent[distance - 1][:, columns] = total.astype(jnp.bfloat16)


def first_sum(place, got, columns):
    return pl.pallas_call(
        first_sum_kernel,
        out_shape=[jax.ShapeDtypeStruct((32, columns), jnp.float32)]
        + [jax.ShapeDtypeStruct((32, columns), jnp.bfloat16)] * 3,
        in_specs=[SMEM, VMEM],
        out_specs=[VMEM] * 4,
        compiler_params=pltpu.CompilerParams(vmem_limit_bytes=20 << 20),
        name="first_sum",
    )(place, got)


def finish_kernel(own, first, second, third, result):
    total = own[...]
    for got in (first, second, third):
        total = total + got[...].astype(jnp.float32)
    result[...] = total.reshape(result.shape)


def finish(own, received):
    return pl.pallas_call(
        finish_kernel,
        out_shape=jax.ShapeDtypeStruct((2, 16, own.shape[1]), jnp.float32),
        in_specs=[VMEM] * 4,
        out_specs=VMEM,
        compiler_params=pltpu.CompilerParams(vmem_limit_bytes=20 << 20),
        name="finish",
    )(own, *received)


def copies(block, count):
    return jnp.broadcast_to(block[None], (count,) + block.shape)


def joined(block, axis, move):
    return jnp.concatenate([block, lax.ppermute(block, axis, move)])


def swap(count, bit):
    return [(i, i ^ bit) for i in range(count)]


def ring(count, distance):
    return [(i, (i + distance) % count) for i in range(count)]


def lane_blocks(rows):
    return rows.reshape(-1, 4, 128).transpose(1, 0, 2).reshape(-1, 128)


def local(token_inputs, frozen_weight, adapter_down_weight, adapter_up_weight):
    core, odd = lax.axis_index("core"), lax.axis_index("yb")
    place = jnp.stack([lax.axis_index(("zb", "ya", "yb")), core, lax.axis_index("zp")])
    place = place.astype(jnp.int32)
    width = frozen_weight.shape[1]

    block = jnp.concatenate(
        [lane_blocks(token_inputs.reshape(32, 512)), lane_blocks(adapter_down_weight.T)]
    )
    block = copies(block, 4)
    block, up = lax.optimization_barrier((block, adapter_up_weight))
    block = lax.all_to_all(block, "zh", 0, 0, tiled=True)
    away = lax.dynamic_slice_in_dim(frozen_weight, (1 - odd) * (width - HALF), HALF, 1)
    partner = lax.ppermute(away, "yb", swap(2, 1))
    up = joined(up, "yb", swap(2, 1))
    up = joined(up, "ya", swap(2, 1))
    up = joined(up, "zb", swap(2, 1))
    up = joined(up, "zp", swap(4, 1))
    up = joined(up, "zp", swap(4, 2))
    block, up, partner = lax.optimization_barrier((block, up, partner))
    own_half = lax.all_to_all(copies(block, 8).reshape(32, 136, 128), ("x", "yb"), 0, 0, tiled=True)
    other_half = lax.ppermute(own_half, "core", swap(2, 1))
    own_half = own_half.reshape(4, 2, 4, 136, 128)
    other_half = other_half.reshape(4, 2, 4, 136, 128)

    sent = products(place, own_half, other_half, up, frozen_weight, partner)
    got = lax.all_to_all(sent, ("zb", "ya", "yb"), 0, 0, tiled=True)
    own, *sent = first_sum(place, got, width)
    received = [lax.ppermute(rows, "zp", ring(4, d)) for d, rows in enumerate(sent, 1)]
    return finish(own, received)


def solution(mesh):
    fine = Mesh(mesh.devices.reshape(SIZES), AXES)
    group, tp = ("x", "zh", "core"), ("zp", "zb", "ya", "yb")
    placed = (P(None, group, tp), P(tp, group), P(tp, group), P(tp, group))
    return jax.shard_map(
        local, mesh=fine, in_specs=placed, out_specs=P(None, tp, group), check_vma=False
    )
```

```python
import jax
import jax.numpy as jnp
from jax import lax
from jax.experimental import pallas as pl
from jax.experimental.pallas import tpu as pltpu
from jax.sharding import Mesh, PartitionSpec as P

adapter_scale = 0.5
RANK = 64
AXES = ("x", "zh", "core", "zp", "zb", "ya", "yb")
SIZES = (4, 4, 2, 4, 2, 2, 2)
HALF = 896
VMEM = pl.BlockSpec(memory_space=pltpu.VMEM)
SMEM = pl.BlockSpec(memory_space=pltpu.SMEM)
TN = (((0,), (0,)), ((), ()))


def partner_half_kernel(place, frozen, away, away_sem):
    start = pl.multiple_of((1 - place[0] % 2) * (frozen.shape[1] - HALF), 128)
    leaving = pltpu.make_async_copy(frozen.at[:, pl.ds(start, HALF)], away, away_sem)
    leaving.start()
    leaving.wait()


def partner_half(place, frozen):
    return pl.pallas_call(
        partner_half_kernel,
        out_shape=jax.ShapeDtypeStruct((frozen.shape[0], HALF), frozen.dtype),
        in_specs=[SMEM, pl.BlockSpec(memory_space=pl.ANY)],
        out_specs=VMEM,
        scratch_shapes=[pltpu.SemaphoreType.DMA],
        name="partner_half",
    )(place, frozen)


def product_kernel(place, own_half, other_half, up, frozen, partner, sent, weight):
    me, core = place[0], place[1]
    odd = me % 2
    columns = pl.ds(pl.multiple_of(odd * (frozen.shape[1] - HALF), 128), HALF)
    row = lax.broadcasted_iota(jnp.int32, (RANK, 256), 0)
    held = lax.broadcasted_iota(jnp.int32, (RANK, 256), 1)
    pair = row >> 1
    source = (pair & 7) ^ me
    x = (pair >> 3) ^ place[2]
    other = (source & 1) ^ core
    first = other * 128 + (x * 4 + (source >> 1)) * 8 + (row & 1)
    picks = [(held == first + 2 * part).astype(jnp.float32).astype(jnp.bfloat16) for part in range(4)]
    up_columns = up[:, columns]
    for whose in range(2):
        features = odd if whose == 0 else 1 - odd
        gathered = jnp.concatenate(
            [half[:, features, :, 128:, :].reshape(128, 128) for half in (own_half, other_half)]
        )
        for part in range(4):
            down = jnp.dot(picks[part], gathered, preferred_element_type=jnp.float32)
            down = down.astype(jnp.bfloat16)
            delta = lax.dot_general(down, up_columns, TN, preferred_element_type=jnp.float32)
            rows = slice(128 * part, 128 * part + 128)
            before = frozen[rows, columns] if whose == 0 else partner[rows, :]
            merged = before.astype(jnp.float32) + adapter_scale * delta
            start = pl.multiple_of(512 * features + 128 * part, 128)
            weight[pl.ds(start, 128), :] = merged.astype(weight.dtype)

    for other, half in enumerate((own_half, other_half)):
        tokens = []
        for zh in range(4):
            lanes = []
            for features in range(2):
                block = half[:, features, zh, :128, :].reshape(4, 4, 32, 128)
                lanes += [block[:, part].reshape(128, 128) for part in range(4)]
            tokens.append(jnp.concatenate(lanes, axis=1))
        tokens = jnp.concatenate(tokens)
        wide = jnp.dot(tokens, weight[...], preferred_element_type=jnp.float32)
        for zh in range(4):
            sent[zh * 2 + (core ^ other)] = wide[128 * zh : 128 * zh + 128, :].astype(sent.dtype)


def products(place, own_half, other_half, up, frozen, partner):
    return pl.pallas_call(
        product_kernel,
        out_shape=jax.ShapeDtypeStruct((8, 128, HALF), jnp.bfloat16),
        in_specs=[SMEM] + [VMEM] * 5,
        out_specs=VMEM,
        scratch_shapes=[pltpu.VMEM((1024, HALF), frozen.dtype)],
        compiler_params=pltpu.CompilerParams(vmem_limit_bytes=20 << 20),
        cost_estimate=pl.CostEstimate(
            flops=2 * 1024 * 1024 * HALF, bytes_accessed=8 << 20, transcendentals=0
        ),
        name="products",
    )(place, own_half, other_half, up, frozen, partner)


def first_sum_kernel(place, got, own, *sent):
    width = own.shape[1]
    for distance in range(4):
        rows = pl.ds(pl.multiple_of(((place[2] + distance) & 3) * 32, 32), 32)
        for odd in range(2):
            lanes = slice(2 * HALF - width, HALF) if odd else slice(0, HALF)
            total = got[odd, rows, lanes].astype(jnp.float32)
            for source in range(odd + 2, 8, 2):
                total = total + got[source, rows, lanes].astype(jnp.float32)
            columns = slice(HALF, width) if odd else slice(0, HALF)
            if distance == 0:
                own[:, columns] = total
            else:
                sent[distance - 1][:, columns] = total.astype(jnp.bfloat16)


def first_sum(place, got, columns):
    return pl.pallas_call(
        first_sum_kernel,
        out_shape=[jax.ShapeDtypeStruct((32, columns), jnp.float32)]
        + [jax.ShapeDtypeStruct((32, columns), jnp.bfloat16)] * 3,
        in_specs=[SMEM, VMEM],
        out_specs=[VMEM] * 4,
        compiler_params=pltpu.CompilerParams(vmem_limit_bytes=20 << 20),
        name="first_sum",
    )(place, got)


def finish_kernel(own, first, second, third, result):
    total = own[...]
    for got in (first, second, third):
        total = total + got[...].astype(jnp.float32)
    result[...] = total.reshape(result.shape)


def finish(own, received):
    return pl.pallas_call(
        finish_kernel,
        out_shape=jax.ShapeDtypeStruct((2, 16, own.shape[1]), jnp.float32),
        in_specs=[VMEM] * 4,
        out_specs=VMEM,
        compiler_params=pltpu.CompilerParams(vmem_limit_bytes=20 << 20),
        name="finish",
    )(own, *received)


def copies(block, count):
    return jnp.broadcast_to(block[None], (count,) + block.shape)


def joined(block, axis, move):
    return jnp.concatenate([block, lax.ppermute(block, axis, move)])


def swap(count, bit):
    return [(i, i ^ bit) for i in range(count)]


def ring(count, distance):
    return [(i, (i + distance) % count) for i in range(count)]


def lane_blocks(rows):
    return rows.reshape(-1, 4, 128).transpose(1, 0, 2).reshape(-1, 128)


def local(token_inputs, frozen_weight, adapter_down_weight, adapter_up_weight):
    core = lax.axis_index("core")
    place = jnp.stack([lax.axis_index(("zb", "ya", "yb")), core, lax.axis_index("zp")])
    place = place.astype(jnp.int32)
    width = frozen_weight.shape[1]

    block = jnp.concatenate(
        [lane_blocks(token_inputs.reshape(32, 512)), lane_blocks(adapter_down_weight.T)]
    )
    block = copies(block, 4)
    block, up = lax.optimization_barrier((block, adapter_up_weight))
    block = lax.all_to_all(block, "zh", 0, 0, tiled=True)
    partner = lax.ppermute(partner_half(place, frozen_weight), "yb", swap(2, 1))
    up = joined(up, "yb", swap(2, 1))
    up = joined(up, "ya", swap(2, 1))
    up = joined(up, "zb", swap(2, 1))
    up = joined(up, "zp", swap(4, 1))
    block, up, partner = lax.optimization_barrier((block, up, partner))
    up = joined(up, "zp", swap(4, 2))
    own_half = lax.all_to_all(copies(block, 8).reshape(32, 136, 128), ("x", "yb"), 0, 0, tiled=True)
    other_half = lax.ppermute(own_half, "core", swap(2, 1))
    own_half = own_half.reshape(4, 2, 4, 136, 128)
    other_half = other_half.reshape(4, 2, 4, 136, 128)

    sent = products(place, own_half, other_half, up, frozen_weight, partner)
    got = lax.all_to_all(sent, ("zb", "ya", "yb"), 0, 0, tiled=True)
    own, *sent = first_sum(place, got, width)
    received = [lax.ppermute(rows, "zp", ring(4, d)) for d, rows in enumerate(sent, 1)]
    return finish(own, received)


def solution(mesh):
    fine = Mesh(mesh.devices.reshape(SIZES), AXES)
    group, tp = ("x", "zh", "core"), ("zp", "zb", "ya", "yb")
    placed = (P(None, group, tp), P(tp, group), P(tp, group), P(tp, group))
    return jax.shard_map(
        local, mesh=fine, in_specs=placed, out_specs=P(None, tp, group), check_vma=False
    )
```

```python
import jax
import jax.numpy as jnp
from jax import lax
from jax.experimental import pallas as pl
from jax.experimental.pallas import tpu as pltpu
from jax.sharding import Mesh, PartitionSpec as P

adapter_scale = 0.5
RANK = 64
AXES = ("x", "zh", "core", "zp", "zb", "ya", "yb")
SIZES = (4, 4, 2, 4, 2, 2, 2)
HALF = 896
VMEM = pl.BlockSpec(memory_space=pltpu.VMEM)
SMEM = pl.BlockSpec(memory_space=pltpu.SMEM)
TN = (((0,), (0,)), ((), ()))


def product_kernel(place, own_half, other_half, up, frozen, partner, sent, weight):
    me, core = place[0], place[1]
    odd = me % 2
    columns = pl.ds(pl.multiple_of(odd * (frozen.shape[1] - HALF), 128), HALF)
    row = lax.broadcasted_iota(jnp.int32, (RANK, 256), 0)
    held = lax.broadcasted_iota(jnp.int32, (RANK, 256), 1)
    pair = row >> 1
    source = (pair & 7) ^ me
    x = (pair >> 3) ^ place[2]
    other = (source & 1) ^ core
    first = other * 128 + (x * 4 + (source >> 1)) * 8 + (row & 1)
    picks = [(held == first + 2 * part).astype(jnp.float32).astype(jnp.bfloat16) for part in range(4)]
    up_columns = up[:, columns]
    for whose in range(2):
        features = odd if whose == 0 else 1 - odd
        gathered = jnp.concatenate(
            [half[:, features, :, 128:, :].reshape(128, 128) for half in (own_half, other_half)]
        )
        for part in range(4):
            down = jnp.dot(picks[part], gathered, preferred_element_type=jnp.float32)
            down = down.astype(jnp.bfloat16)
            delta = lax.dot_general(down, up_columns, TN, preferred_element_type=jnp.float32)
            rows = slice(128 * part, 128 * part + 128)
            before = frozen[rows, columns] if whose == 0 else partner[rows, :]
            merged = before.astype(jnp.float32) + adapter_scale * delta
            start = pl.multiple_of(512 * features + 128 * part, 128)
            weight[pl.ds(start, 128), :] = merged.astype(weight.dtype)

    for other, half in enumerate((own_half, other_half)):
        tokens = []
        for zh in range(4):
            lanes = []
            for features in range(2):
                block = half[:, features, zh, :128, :].reshape(4, 4, 32, 128)
                lanes += [block[:, part].reshape(128, 128) for part in range(4)]
            tokens.append(jnp.concatenate(lanes, axis=1))
        tokens = jnp.concatenate(tokens)
        wide = jnp.dot(tokens, weight[...], preferred_element_type=jnp.float32)
        for zh in range(4):
            sent[zh * 2 + (core ^ other)] = wide[128 * zh : 128 * zh + 128, :].astype(sent.dtype)


def products(place, own_half, other_half, up, frozen, partner):
    return pl.pallas_call(
        product_kernel,
        out_shape=jax.ShapeDtypeStruct((8, 128, HALF), jnp.bfloat16),
        in_specs=[SMEM] + [VMEM] * 5,
        out_specs=VMEM,
        scratch_shapes=[pltpu.VMEM((1024, HALF), frozen.dtype)],
        compiler_params=pltpu.CompilerParams(vmem_limit_bytes=20 << 20),
        cost_estimate=pl.CostEstimate(
            flops=2 * 1024 * 1024 * HALF, bytes_accessed=8 << 20, transcendentals=0
        ),
        name="products",
    )(place, own_half, other_half, up, frozen, partner)


def first_sum_kernel(place, got, own, *sent):
    width = own.shape[1]
    for distance in range(4):
        rows = pl.ds(pl.multiple_of(((place[2] + distance) & 3) * 32, 32), 32)
        for odd in range(2):
            lanes = slice(2 * HALF - width, HALF) if odd else slice(0, HALF)
            total = got[odd, rows, lanes].astype(jnp.float32)
            for source in range(odd + 2, 8, 2):
                total = total + got[source, rows, lanes].astype(jnp.float32)
            columns = slice(HALF, width) if odd else slice(0, HALF)
            if distance == 0:
                own[:, columns] = total
            else:
                sent[distance - 1][:, columns] = total.astype(jnp.bfloat16)


def first_sum(place, got, columns):
    return pl.pallas_call(
        first_sum_kernel,
        out_shape=[jax.ShapeDtypeStruct((32, columns), jnp.float32)]
        + [jax.ShapeDtypeStruct((32, columns), jnp.bfloat16)] * 3,
        in_specs=[SMEM, VMEM],
        out_specs=[VMEM] * 4,
        compiler_params=pltpu.CompilerParams(vmem_limit_bytes=20 << 20),
        name="first_sum",
    )(place, got)


def finish_kernel(own, first, second, third, result):
    total = own[...]
    for got in (first, second, third):
        total = total + got[...].astype(jnp.float32)
    result[...] = total.reshape(result.shape)


def finish(own, received):
    return pl.pallas_call(
        finish_kernel,
        out_shape=jax.ShapeDtypeStruct((2, 16, own.shape[1]), jnp.float32),
        in_specs=[VMEM] * 4,
        out_specs=VMEM,
        compiler_params=pltpu.CompilerParams(vmem_limit_bytes=20 << 20),
        name="finish",
    )(own, *received)


def copies(block, count):
    return jnp.broadcast_to(block[None], (count,) + block.shape)


def joined(block, axis, move):
    return jnp.concatenate([block, lax.ppermute(block, axis, move)])


def swap(count, bit):
    return [(i, i ^ bit) for i in range(count)]


def ring(count, distance):
    return [(i, (i + distance) % count) for i in range(count)]


def lane_blocks(rows):
    return rows.reshape(-1, 4, 128).transpose(1, 0, 2).reshape(-1, 128)


def local(token_inputs, frozen_weight, adapter_down_weight, adapter_up_weight):
    core, odd = lax.axis_index("core"), lax.axis_index("yb")
    place = jnp.stack([lax.axis_index(("zb", "ya", "yb")), core, lax.axis_index("zp")])
    place = place.astype(jnp.int32)
    width = frozen_weight.shape[1]

    block = jnp.concatenate(
        [lane_blocks(token_inputs.reshape(32, 512)), lane_blocks(adapter_down_weight.T)]
    )
    block = copies(block, 4)
    block, up = lax.optimization_barrier((block, adapter_up_weight))
    block = lax.all_to_all(block, "zh", 0, 0, tiled=True)
    away = lax.dynamic_slice_in_dim(frozen_weight, (1 - odd) * (width - HALF), HALF, 1)
    partner = lax.ppermute(away, "yb", swap(2, 1))
    up = joined(up, "yb", swap(2, 1))
    up = joined(up, "ya", swap(2, 1))
    up = joined(up, "zb", swap(2, 1))
    up = joined(up, "zp", swap(4, 1))
    block, up, partner = lax.optimization_barrier((block, up, partner))
    up = joined(up, "zp", swap(4, 2))
    own_half = lax.all_to_all(copies(block, 8).reshape(32, 136, 128), ("x", "yb"), 0, 0, tiled=True)
    own_half, up = lax.optimization_barrier((own_half, up))
    other_half = lax.ppermute(own_half, "core", swap(2, 1))
    own_half = own_half.reshape(4, 2, 4, 136, 128)
    other_half = other_half.reshape(4, 2, 4, 136, 128)

    sent = products(place, own_half, other_half, up, frozen_weight, partner)
    got = lax.all_to_all(sent, ("zb", "ya", "yb"), 0, 0, tiled=True)
    own, *sent = first_sum(place, got, width)
    received = [lax.ppermute(rows, "zp", ring(4, d)) for d, rows in enumerate(sent, 1)]
    return finish(own, received)


def solution(mesh):
    fine = Mesh(mesh.devices.reshape(SIZES), AXES)
    group, tp = ("x", "zh", "core"), ("zp", "zb", "ya", "yb")
    placed = (P(None, group, tp), P(tp, group), P(tp, group), P(tp, group))
    return jax.shard_map(
        local, mesh=fine, in_specs=placed, out_specs=P(None, tp, group), check_vma=False
    )
```

```python
import jax
import jax.numpy as jnp
from jax import lax
from jax.experimental import pallas as pl
from jax.experimental.pallas import tpu as pltpu
from jax.sharding import Mesh, PartitionSpec as P

adapter_scale = 0.5
RANK = 64
AXES = ("x", "zh", "core", "zp", "zb", "ya", "yb")
SIZES = (4, 4, 2, 4, 2, 2, 2)
HALF = 896
VMEM = pl.BlockSpec(memory_space=pltpu.VMEM)
SMEM = pl.BlockSpec(memory_space=pltpu.SMEM)
TN = (((0,), (0,)), ((), ()))


def product_kernel(place, own_half, other_half, up, frozen, partner, kept, *sent):
    *sent, weight = sent
    me, core = place[0], place[1]
    odd = me % 2
    columns = pl.ds(pl.multiple_of(odd * (frozen.shape[1] - HALF), 128), HALF)
    row = lax.broadcasted_iota(jnp.int32, (RANK, 256), 0)
    held = lax.broadcasted_iota(jnp.int32, (RANK, 256), 1)
    pair = row >> 1
    source = (pair & 7) ^ me
    x = (pair >> 3) ^ place[2]
    other = (source & 1) ^ core
    first = other * 128 + (x * 4 + (source >> 1)) * 8 + (row & 1)
    picks = [(held == first + 2 * part).astype(jnp.float32).astype(jnp.bfloat16) for part in range(4)]
    up_columns = up[:, columns]
    for whose in range(2):
        features = odd if whose == 0 else 1 - odd
        gathered = jnp.concatenate(
            [half[:, features, :, 128:, :].reshape(128, 128) for half in (own_half, other_half)]
        )
        for part in range(4):
            down = jnp.dot(picks[part], gathered, preferred_element_type=jnp.float32)
            down = down.astype(jnp.bfloat16)
            delta = lax.dot_general(down, up_columns, TN, preferred_element_type=jnp.float32)
            rows = slice(128 * part, 128 * part + 128)
            before = frozen[rows, columns] if whose == 0 else partner[rows, :]
            merged = before.astype(jnp.float32) + adapter_scale * delta
            start = pl.multiple_of(512 * features + 128 * part, 128)
            weight[pl.ds(start, 128), :] = merged.astype(weight.dtype)

    for mask in range(8):
        target = me ^ mask
        zh, theirs = target >> 1, ((target & 1) ^ core) == 1
        tokens = []
        for features in range(2):
            block = jnp.where(
                theirs, other_half[:, features, zh, :128, :], own_half[:, features, zh, :128, :]
            ).reshape(4, 4, 32, 128)
            tokens += [block[:, part].reshape(128, 128) for part in range(4)]
        tokens = jnp.concatenate(tokens, axis=1)
        wide = jnp.dot(tokens, weight[...], preferred_element_type=jnp.float32)
        if mask == 0:
            kept[...] = wide
        else:
            sent[mask - 1][...] = wide.astype(jnp.bfloat16)


def products(place, own_half, other_half, up, frozen, partner):
    return pl.pallas_call(
        product_kernel,
        out_shape=[jax.ShapeDtypeStruct((128, HALF), jnp.float32)]
        + [jax.ShapeDtypeStruct((128, HALF), jnp.bfloat16)] * 7,
        in_specs=[SMEM] + [VMEM] * 5,
        out_specs=[VMEM] * 8,
        scratch_shapes=[pltpu.VMEM((1024, HALF), frozen.dtype)],
        compiler_params=pltpu.CompilerParams(vmem_limit_bytes=20 << 20),
        cost_estimate=pl.CostEstimate(
            flops=2 * 1024 * 1024 * HALF, bytes_accessed=8 << 20, transcendentals=0
        ),
        name="products",
    )(place, own_half, other_half, up, frozen, partner)


def first_sum_kernel(place, kept, *refs):
    got, own, sent = refs[:7], refs[7], refs[8:]
    width = own.shape[1]
    even = place[0] % 2 == 0
    for distance in range(4):
        rows = pl.ds(pl.multiple_of(((place[2] + distance) & 3) * 32, 32), 32)
        same, others = kept[rows, :], got[0][rows, :].astype(jnp.float32)
        for mask in range(2, 8):
            part = got[mask - 1][rows, :].astype(jnp.float32)
            same, others = (same, others + part) if mask % 2 else (same + part, others)
        left = jnp.where(even, same, others)
        right = jnp.where(even, others, same)[:, 2 * HALF - width :]
        into = own if distance == 0 else sent[distance - 1]
        into[:, :HALF] = left.astype(into.dtype)
        into[:, HALF:] = right.astype(into.dtype)


def first_sum(place, kept, got, columns):
    return pl.pallas_call(
        first_sum_kernel,
        out_shape=[jax.ShapeDtypeStruct((32, columns), jnp.float32)]
        + [jax.ShapeDtypeStruct((32, columns), jnp.bfloat16)] * 3,
        in_specs=[SMEM] + [VMEM] * 8,
        out_specs=[VMEM] * 4,
        compiler_params=pltpu.CompilerParams(vmem_limit_bytes=20 << 20),
        name="first_sum",
    )(place, kept, *got)


def finish_kernel(own, first, second, third, result):
    total = own[...]
    for got in (first, second, third):
        total = total + got[...].astype(jnp.float32)
    result[...] = total.reshape(result.shape)


def finish(own, received):
    return pl.pallas_call(
        finish_kernel,
        out_shape=jax.ShapeDtypeStruct((2, 16, own.shape[1]), jnp.float32),
        in_specs=[VMEM] * 4,
        out_specs=VMEM,
        compiler_params=pltpu.CompilerParams(vmem_limit_bytes=20 << 20),
        name="finish",
    )(own, *received)


def copies(block, count):
    return jnp.broadcast_to(block[None], (count,) + block.shape)


def joined(block, axis, move):
    return jnp.concatenate([block, lax.ppermute(block, axis, move)])


def swap(count, bit):
    return [(i, i ^ bit) for i in range(count)]


def ring(count, distance):
    return [(i, (i + distance) % count) for i in range(count)]


def lane_blocks(rows):
    return rows.reshape(-1, 4, 128).transpose(1, 0, 2).reshape(-1, 128)


def local(token_inputs, frozen_weight, adapter_down_weight, adapter_up_weight):
    core, odd = lax.axis_index("core"), lax.axis_index("yb")
    place = jnp.stack([lax.axis_index(("zb", "ya", "yb")), core, lax.axis_index("zp")])
    place = place.astype(jnp.int32)
    width = frozen_weight.shape[1]

    block = jnp.concatenate(
        [lane_blocks(token_inputs.reshape(32, 512)), lane_blocks(adapter_down_weight.T)]
    )
    block = copies(block, 4)
    block, up = lax.optimization_barrier((block, adapter_up_weight))
    block = lax.all_to_all(block, "zh", 0, 0, tiled=True)
    away = lax.dynamic_slice_in_dim(frozen_weight, (1 - odd) * (width - HALF), HALF, 1)
    partner = lax.ppermute(away, "yb", swap(2, 1))
    up = joined(up, "yb", swap(2, 1))
    up = joined(up, "ya", swap(2, 1))
    up = joined(up, "zb", swap(2, 1))
    up = joined(up, "zp", swap(4, 1))
    block, up, partner = lax.optimization_barrier((block, up, partner))
    up = joined(up, "zp", swap(4, 2))
    own_half = lax.all_to_all(copies(block, 8).reshape(32, 136, 128), ("x", "yb"), 0, 0, tiled=True)
    own_half, up = lax.optimization_barrier((own_half, up))
    other_half = lax.ppermute(own_half, "core", swap(2, 1))
    own_half = own_half.reshape(4, 2, 4, 136, 128)
    other_half = other_half.reshape(4, 2, 4, 136, 128)

    kept, *sent = products(place, own_half, other_half, up, frozen_weight, partner)
    got = [lax.ppermute(rows, ("zb", "ya", "yb"), swap(8, mask)) for mask, rows in enumerate(sent, 1)]
    own, *sent = first_sum(place, kept, got, width)
    received = [lax.ppermute(rows, "zp", ring(4, d)) for d, rows in enumerate(sent, 1)]
    return finish(own, received)


def solution(mesh):
    fine = Mesh(mesh.devices.reshape(SIZES), AXES)
    group, tp = ("x", "zh", "core"), ("zp", "zb", "ya", "yb")
    placed = (P(None, group, tp), P(tp, group), P(tp, group), P(tp, group))
    return jax.shard_map(
        local, mesh=fine, in_specs=placed, out_specs=P(None, tp, group), check_vma=False
    )
```
